32 devices in a mesh: row: 4 (over z), col: 8 (over y, x, core).
Axes of the slice: x: 2, y: 2, z: 4, core: 2. Of those that a mesh axis runs over, the one named last changes fastest.
Arguments:
- front: float32 [62464, 1024], P('row', 'col')
- child_update: bfloat16 [62464, 1024], P('row', 'col'), may hold values from -6 to 6
- child_rows: int32 [4, 244], replicated, may hold values from 8 to 487, as said below
Outputs:
- factor: float32 [62464, 1024], P('row', 'col')
The draws below stay inside these ranges and needn't reach their ends.
Inputs may be any that keep to these rules, and one draw needn't show every extreme that they name: `child_rows`: each row names 244 distinct parent block rows, none below 8. Block row b of child c lies on row group (c // 2) * 2 + b // 122; the 122 block rows of one row group go to the parent row groups (each owning 122 consecutive block rows) in turn, from a drawn first one, so at most 31 of them reach one parent row group.
All inputs are finite; a program needn't handle non-finite values.
Results may differ from the reference program's by a relative error of at most 0.0017.
Values may be sent and summed in bfloat16 or wider, within the bound.
A program may use at most 128 MiB of HBM per device.

```python
import math
import jax
import jax.numpy as jnp

BLOCK = 128
NF = 62464
CR = 31232
STEPS = 3
WC = 1024
TOPB = 8
NGROUPS = 4
HALFG = 2
ROWB = 122
RBC = 122


def draw_front(key, part):
    key_lower = jax.random.fold_in(key, 11)
    key_points = jax.random.fold_in(key, 12)
    key_flip = jax.random.fold_in(key, 13)
    key_scale = jax.random.fold_in(key, 14)
    side_length = math.sqrt(WC)
    points = jax.random.uniform(key_points, (WC, 2), jnp.float32, 0.0, side_length)
    delta_x = points[:, 0][:, None] - points[:, 0][None, :]
    delta_y = points[:, 1][:, None] - points[:, 1][None, :]
    distance = jnp.sqrt(delta_x * delta_x + delta_y * delta_y)
    kernel = jnp.exp(-distance / 1.5)
    scales = jnp.exp(jax.random.uniform(key_scale, (WC,), jnp.float32, jnp.log(0.8), jnp.log(1.25)))
    sign_flip = jnp.where(jax.random.bernoulli(key_flip, 0.5, (WC,)), 1.0, -1.0).astype(jnp.float32)
    lower_rows = jnp.clip(jax.random.normal(key_lower, (NF - WC, WC), jnp.float32), -6.0, 6.0)
    weight = scales * sign_flip
    top_square = weight[:, None] * kernel * weight[None, :] + 0.5 * jnp.eye(WC, dtype=jnp.float32)
    return jnp.concatenate([top_square, lower_rows], axis=0).astype(jnp.float32)


def draw_child_rows(key, part):
    offsets = jax.random.randint(jax.random.fold_in(key, 1), (4, HALFG), 0, NGROUPS)
    positions = jnp.arange(RBC, dtype=jnp.int32)
    group_ids = jnp.arange(NGROUPS, dtype=jnp.int32)
    results = []
    for child_id in range(4):
        targets = (positions[None, :] + offsets[child_id][:, None]) % NGROUPS
        flat_targets = targets.reshape(-1)
        one_hot = (flat_targets[:, None] == group_ids[None, :]).astype(jnp.int32)
        ranking = jnp.sum((jnp.cumsum(one_hot, axis=0) - one_hot) * one_hot, axis=1)
        tables = []
        for group_id in range(NGROUPS):
            group_key = jax.random.fold_in(jax.random.fold_in(key, 100 + child_id), group_id)
            if group_id == 0:
                choose = TOPB + jax.random.permutation(group_key, ROWB - TOPB)
            else:
                choose = jax.random.permutation(group_key, ROWB)[:ROWB - TOPB]
            tables.append(group_id * ROWB + choose.astype(jnp.int32))
        table_all = jnp.stack(tables)
        results.append(table_all[flat_targets, ranking])
    return jnp.stack(results).astype(jnp.int32)


def block_levels(rng, dims, shards, least, largest):
    def one(axis_at, shards_of):
        draws = jax.random.uniform(jax.random.fold_in(jax.random.fold_in(rng, 6), axis_at), (shards_of,), jnp.float32, least / len(shards), largest / len(shards))
        return jnp.repeat(jnp.exp(draws), dims[axis_at] // shards_of).reshape((-1,) + (1,) * (len(dims) - axis_at - 1))

    gain = one(*shards[0])
    for cut in shards[1:]:
        gain = gain * one(*cut)
    return gain


def gaussian(rng, shape, spread, limit, pieces=(), held_as=jnp.bfloat16):
    loudness = block_levels(rng, shape, pieces, -0.22, 0.18) if pieces else 1.0
    values = jax.random.normal(rng, shape, jnp.float32) * spread * loudness
    return jnp.minimum(jnp.maximum(values, -limit), limit).astype(held_as)


def setup_inputs(seed: int = 0) -> dict:
    key_of = jax.random.split(jax.random.key(seed), 4)
    return {
        "front": draw_front(jax.random.fold_in(key_of[3], 71), 0),
        "child_update": gaussian(key_of[1], (2 * CR, WC), 1.0, 6.0, ((0, 4), (1, 8))),
        "child_rows": draw_child_rows(jax.random.fold_in(key_of[3], 71), 0),
    }


def reference(front, child_update, child_rows):
    half_cols = WC // 2
    assembled = front
    for child_id in range(4):
        row_half = child_id // 2
        col_half = child_id % 2
        block_part = child_update[row_half * CR:(row_half + 1) * CR, col_half * half_cols:(col_half + 1) * half_cols].astype(jnp.float32)
        target_rows = (child_rows[child_id][:, None] * BLOCK + jnp.arange(BLOCK, dtype=jnp.int32)[None, :]).reshape(-1)
        assembled = assembled.at[target_rows, col_half * half_cols:(col_half + 1) * half_cols].add(block_part)
    working = assembled
    row_ids = jnp.arange(NF, dtype=jnp.int32)[:, None]
    factor = jnp.zeros((NF, WC), jnp.float32)
    for panel_step in range(STEPS):
        first_col = panel_step * BLOCK
        corner = working[first_col:first_col + BLOCK, first_col:first_col + BLOCK]
        symmetric = jnp.tril(corner) + jnp.tril(corner, -1).T
        lower_factor = jnp.linalg.cholesky(symmetric)
        solved = jax.scipy.linalg.solve_triangular(lower_factor, working[:, first_col:first_col + BLOCK].T, lower=True).T
        placed = jnp.zeros((NF, BLOCK), jnp.float32).at[first_col:first_col + BLOCK].set(lower_factor)
        panel_cols = jnp.where(row_ids < first_col, 0.0, jnp.where(row_ids < first_col + BLOCK, placed, solved))
        factor = factor.at[:, first_col:first_col + BLOCK].set(panel_cols)
        narrow = panel_cols.astype(jnp.bfloat16)
        if first_col + BLOCK < WC:
            update = jnp.dot(narrow.astype(jnp.float32), narrow[first_col + BLOCK:WC].T.astype(jnp.float32), preferred_element_type=jnp.float32)
            working = working.at[:, first_col + BLOCK:].add(-update)
    rest_cols = STEPS * BLOCK
    if rest_cols < WC:
        factor = factor.at[:, rest_cols:].set(working[:, rest_cols:])
    col_ids = jnp.arange(WC, dtype=jnp.int32)[None, :]
    return jnp.where(row_ids >= col_ids, factor, 0.0)
```

```python
import functools

import jax
import jax.numpy as jnp
from jax import lax
from jax.experimental import pallas as pl
from jax.experimental.pallas import tpu as pltpu
from jax.sharding import PartitionSpec as P

STEPS = 3
MESH = pl.DeviceIdType.MESH
EXACT = lax.Precision.HIGHEST
F32 = jnp.float32
BF16 = jnp.bfloat16


def dot_t(a, b, precision=None):
    return lax.dot_general(
        a, b, (((1,), (1,)), ((), ())), precision=precision, preferred_element_type=F32
    )


def tables_kernel(groups, blocks, cap, ids_ref, send_ref, take_ref, count_ref):
    me = lax.axis_index("row")
    half = groups // 2
    col_half = lax.axis_index("col") // (lax.axis_size("col") // 2)

    def clear_send(i, _):
        send_ref[i] = 0
        return 0

    def clear_take(i, _):
        take_ref[i] = groups * cap
        return 0

    lax.fori_loop(0, groups * cap, clear_send, 0)
    lax.fori_loop(0, 2 * blocks, clear_take, 0)
    for g in range(groups):
        count_ref[g] = 0
    mine = 2 * (me // half) + col_half
    mine_first = (me % half) * blocks

    def pack(b, _):
        target = lax.div(ids_ref[mine, mine_first + b], jnp.int32(blocks))
        slot = count_ref[target]
        count_ref[target] = slot + 1
        send_ref[target * cap + slot] = b
        return 0

    lax.fori_loop(0, blocks, pack, 0)
    low = me * blocks
    for g in range(groups):
        child = 2 * (g // half) + col_half
        first = (g % half) * blocks

        def take(b, slot):
            local = ids_ref[child, first + b] - low
            here = (local >= 0) & (local < blocks)

            @pl.when(here)
            def _():
                take_ref[(g // half) * blocks + local] = g * cap + slot

            return slot + here.astype(jnp.int32)

        lax.fori_loop(0, blocks, take, jnp.int32(0))


def routes(chips):
    every = (0, 1, 2, 3)
    if chips == 4:
        wide = [
            (0, 1, (1, 2, 3)),
            (0, 2, (0, 2, 3)),
            (2, 3, (0, 2, 3)),
            (3, 1, (0,)),
            (1, 3, (1,)),
            (3, 2, (1,)),
        ]
        return [wide, wide, [(1, 3, every), (3, 2, every)]]
    return [
        [(q, q + 1, every) for q in range(p // 2, chips - 1)] for p in range(STEPS)
    ]


def front_kernel(
    groups, cols, blocks, cap, chunk, front_ref, child_ref, send_ref, take_ref, out_ref,
    outgoing, incoming, narrow, top, square, lower, inverse, facing, my_inverse,
    local_sem, ex_send, ex_recv, top_send, top_recv, fac_send, fac_recv, pan_send, pan_recv,
):
    block = 128
    head = STEPS * block
    row = lax.axis_index("row")
    col = lax.axis_index("col")
    chip = col // 2
    core = col % 2
    chunks = blocks * block // chunk
    per_chunk = (blocks + chunks - 1) // chunks

    barrier = pltpu.get_barrier_semaphore()

    def greet_row(o, _):
        pl.semaphore_signal(
            barrier, inc=1, device_id={"row": (row + o) % groups}, device_id_type=MESH
        )
        return 0

    def greet_col(o, _):
        pl.semaphore_signal(
            barrier, inc=1, device_id={"col": (col + o) % cols}, device_id_type=MESH
        )
        return 0

    lax.fori_loop(1, groups, greet_row, 0)
    lax.fori_loop(1, cols, greet_col, 0)
    load = pltpu.make_async_copy(front_ref, out_ref, local_sem.at[0])
    load.start()

    def pack(o, dest):
        base = (row + o) % groups * cap

        def one(s, _):
            dest(s, child_ref[send_ref[base + s]])
            return 0

        lax.fori_loop(0, cap, one, 0)

    def to_self(s, tile):
        incoming[row * cap + s] = tile

    def exchange(o):
        return pltpu.make_async_remote_copy(
            src_ref=outgoing.at[o - 1],
            dst_ref=incoming.at[pl.ds(row * cap, cap)],
            send_sem=ex_send.at[o - 1],
            recv_sem=ex_recv.at[o - 1],
            device_id={"row": (row + o) % groups},
            device_id_type=MESH,
        )

    def top_copies(p, j):
        return [
            pltpu.make_async_remote_copy(
                src_ref=front_ref.at[pl.ds(0, head)],
                dst_ref=top.at[p, pl.ds(0, head)],
                send_sem=top_send.at[0, j],
                recv_sem=top_recv.at[0, p],
                device_id={"col": j},
                device_id_type=MESH,
            ),
            pltpu.make_async_remote_copy(
                src_ref=front_ref.at[pl.ds(pl.multiple_of(j * block, block), block)],
                dst_ref=top.at[p, pl.ds(head, block)],
                send_sem=top_send.at[1, j],
                recv_sem=top_recv.at[1, p],
                device_id={"col": j},
                device_id_type=MESH,
            ),
        ]

    def top_local(p):
        return [
            pltpu.make_async_copy(
                front_ref.at[pl.ds(0, head)], top.at[p, pl.ds(0, head)], local_sem.at[1]
            ),
            pltpu.make_async_copy(
                front_ref.at[pl.ds(pl.multiple_of(col * block, block), block)],
                top.at[p, pl.ds(head, block)],
                local_sem.at[2],
            ),
        ]

    pl.semaphore_wait(barrier, groups - 1 + cols - 1)
    for p in range(STEPS):

        @pl.when((row == 0) & (col == p))
        def _():
            for copy in top_local(p):
                copy.start()

            def send(o, _):
                for copy in top_copies(p, (col + o) % cols):
                    copy.start()
                return 0

            lax.fori_loop(1, cols, send, 0)

    for o in range(1, groups):

        def to_out(s, tile, o=o):
            outgoing[o - 1, s] = tile

        pack(o, to_out)
        exchange(o).start()
    pack(0, to_self)
    incoming[groups * cap] = jnp.zeros((block, block), BF16)

    def give(o, ref, at):
        return pltpu.make_async_remote_copy(
            src_ref=ref,
            dst_ref=ref,
            send_sem=fac_send.at[at, o - 1],
            recv_sem=fac_recv.at[at],
            device_id={"row": o},
            device_id_type=MESH,
        )

    lane = lax.broadcasted_iota(jnp.int32, (block, block), 1)
    sub = lax.broadcasted_iota(jnp.int32, (block, block), 0)

    @pl.when(row == 0)
    def _():
        for p in range(STEPS):

            @pl.when(col == p)
            def _():
                for copy in top_local(p):
                    copy.wait()

            @pl.when(col != p)
            def _():
                for copy in top_copies(p, col):
                    copy.wait_recv()

        my_inverse[...] = jnp.zeros((block, block), F32)
        for k in range(STEPS):
            here = pl.ds(k * block, block)
            corner = top[k, here]
            square[...] = jnp.where(sub >= lane, corner, corner.T)
            inverse[...] = jnp.where(sub == lane, 1.0, 0.0).astype(F32)

            def eliminate(i, _):
                whole = square[...]
                pivot = square[pl.ds(i, 1), :]
                unit = inverse[pl.ds(i, 1), :]
                diag = jnp.sum(jnp.where(lane[:1] == i, pivot, 0.0), axis=1, keepdims=True)
                root = jnp.sqrt(diag)
                pivot = pivot / root
                unit = unit / root
                column = jnp.sum(jnp.where(lane == i, whole, 0.0), axis=1, keepdims=True) / root
                column = jnp.where(sub[:, :1] > i, column, 0.0)
                square[...] = jnp.where(sub == i, pivot, whole - column * pivot)
                inverse[...] = jnp.where(sub == i, unit, inverse[...] - column * unit)
                return 0

            lax.fori_loop(0, block, eliminate, 0)
            inv = inverse[...]

            @pl.when(col == k)
            def _():
                lower[...] = jnp.where(lane >= sub, square[...], 0.0).T
                my_inverse[...] = inv

            rounded = dot_t(top[k], inv, EXACT).astype(BF16)
            facing[k] = rounded[head:]
            for later in range(k + 1, STEPS):
                top[later] = top[later] - dot_t(
                    rounded, rounded[later * block : (later + 1) * block]
                )

        def hand_on(o, _):
            give(o, facing, 0).start()
            give(o, my_inverse, 1).start()
            return 0

        lax.fori_loop(1, groups, hand_on, 0)

    @pl.when(row != 0)
    def _():
        give(1, facing, 0).wait_recv()
        give(1, my_inverse, 1).wait_recv()

    for o in range(1, groups):
        exchange(o).wait_recv()
    load.wait()

    plan = routes(cols // 2)

    def panel_copy(p, c, edge, to):
        part = narrow.at[p, pl.ds(pl.multiple_of(c * chunk, 16), chunk)]
        return pltpu.make_async_remote_copy(
            src_ref=part,
            dst_ref=part,
            send_sem=pan_send.at[p, edge, c],
            recv_sem=pan_recv.at[p, c],
            device_id={"col": to},
            device_id_type=MESH,
        )

    def for_sends(p, c, action):
        @pl.when(core == p % 2)
        def _():
            number = {}
            for source, to, classes in plan[p]:
                edge = number.get(source, 0)
                number[source] = edge + 1
                wanted = chip == source
                if len(classes) < 4:
                    kind = c % 4
                    wanted &= functools.reduce(
                        lambda a, b: a | b, [kind == x for x in classes]
                    )

                @pl.when(wanted)
                def _():
                    action(panel_copy(p, c, edge, to * 2 + core))

            sibling = chip > p // 2 if p % 2 else chip >= p // 2

            @pl.when(sibling)
            def _():
                action(panel_copy(p, c, 2, col + 1 - 2 * core))

    def send(p, c):
        for_sends(p, c, lambda copy: copy.start())

    def arrived(p, c):
        panel_copy(p, c, 0, 0).wait_recv()

    def assemble(c):
        def one(b, _):
            r = c * per_chunk + b

            @pl.when(r < blocks)
            def _():
                at = pl.ds(pl.multiple_of(r * block, block), block)
                out_ref[at] = (
                    out_ref[at]
                    + incoming[take_ref[r]].astype(F32)
                    + incoming[take_ref[blocks + r]].astype(F32)
                )

            return 0

        lax.fori_loop(0, per_chunk, one, 0)

    def update(c, count):
        at = pl.ds(pl.multiple_of(c * chunk, 16), chunk)
        value = out_ref[at]
        for p in range(count):
            value = value - dot_t(narrow[p, at], facing[p])
        if count < STEPS:
            pass
        return at, value

    def solve(c, p):
        at, value = update(c, p)
        value = dot_t(value, my_inverse[...], EXACT)
        narrow[p, at] = value.astype(BF16)
        out_ref[at] = value
        send(p, c)

    lag = jnp.where(col < 4, 1, 4)

    def step(s, _):
        @pl.when(s < chunks)
        def _():
            assemble(s)

            @pl.when(col == 0)
            def _():
                solve(s, 0)

            @pl.when((core == 0) & (col > 0))
            def _():
                arrived(0, s)
                send(0, s)

            @pl.when(col == 1)
            def _():
                arrived(0, s)
                solve(s, 1)

            @pl.when((core == 1) & (col > 1))
            def _():
                arrived(1, s)
                send(1, s)

        c = s - lag

        @pl.when((c >= 0) & (c < chunks))
        def _():
            @pl.when((core == 0) & (col > 1))
            def _():
                arrived(1, c)

            @pl.when((core == 1) & (col > 1))
            def _():
                arrived(0, c)

            @pl.when(col == 2)
            def _():
                solve(c, 2)

            @pl.when(col > 2)
            def _():
                arrived(2, c)

                @pl.when(core == 0)
                def _():
                    send(2, c)

                at, value = update(c, STEPS)
                out_ref[at] = value

        return 0

    lax.fori_loop(0, chunks + 4, step, 0)

    @pl.when(row == 0)
    def _():
        def clear(i, _):
            at = pl.ds(pl.multiple_of(i * block, block), block)

            @pl.when(i < col)
            def _():
                out_ref[at] = jnp.zeros((block, block), F32)

            @pl.when((i == col) & (col < STEPS))
            def _():
                out_ref[at] = lower[...]

            @pl.when((i == col) & (col >= STEPS))
            def _():
                out_ref[at] = jnp.where(sub >= lane, out_ref[at], 0.0)

            return 0

        lax.fori_loop(0, cols, clear, 0)

    for o in range(1, groups):
        exchange(o).wait_send()

    @pl.when(row == 0)
    def _():
        def gone(o, _):
            give(o, facing, 0).wait_send()
            give(o, my_inverse, 1).wait_send()
            return 0

        lax.fori_loop(1, groups, gone, 0)
        for p in range(STEPS):

            @pl.when(col == p)
            def _():
                def left(o, _):
                    for copy in top_copies(p, (col + o) % cols):
                        copy.wait_send()
                    return 0

                lax.fori_loop(1, cols, left, 0)

    def drain(c, _):
        for p in range(STEPS):

            @pl.when(col >= p)
            def _():
                for_sends(p, c, lambda copy: copy.wait_send())

        return 0

    lax.fori_loop(0, chunks, drain, 0)


def on_device(front, child_update, child_rows):
    rows, block = front.shape
    groups = lax.axis_size("row")
    cols = lax.axis_size("col")
    blocks = rows // block
    cap = (blocks + groups - 1) // groups
    chunk = max(c for c in range(16, 1025, 16) if rows % c == 0)
    chunks = rows // chunk
    send, take = pl.pallas_call(
        functools.partial(tables_kernel, groups, blocks, cap),
        out_shape=(
            jax.ShapeDtypeStruct((groups * cap,), jnp.int32),
            jax.ShapeDtypeStruct((2 * blocks,), jnp.int32),
        ),
        in_specs=[pl.BlockSpec(memory_space=pltpu.SMEM)],
        out_specs=(
            pl.BlockSpec(memory_space=pltpu.SMEM),
            pl.BlockSpec(memory_space=pltpu.SMEM),
        ),
        scratch_shapes=[pltpu.SMEM((groups,), jnp.int32)],
    )(child_rows)
    dma = pltpu.SemaphoreType.DMA
    return pl.pallas_call(
        functools.partial(front_kernel, groups, cols, blocks, cap, chunk),
        out_shape=jax.ShapeDtypeStruct((rows, block), F32),
        in_specs=[
            pl.BlockSpec(memory_space=pl.ANY),
            pl.BlockSpec(memory_space=pltpu.VMEM),
            pl.BlockSpec(memory_space=pltpu.SMEM),
            pl.BlockSpec(memory_space=pltpu.SMEM),
        ],
        out_specs=pl.BlockSpec(memory_space=pltpu.VMEM),
        scratch_shapes=[
            pltpu.VMEM((groups - 1, cap, block, block), BF16),
            pltpu.VMEM((groups * cap + 1, block, block), BF16),
            pltpu.VMEM((STEPS, rows, block), BF16),
            pltpu.VMEM((STEPS, (STEPS + 1) * block, block), F32),
            pltpu.VMEM((block, block), F32),
            pltpu.VMEM((block, block), F32),
            pltpu.VMEM((block, block), F32),
            pltpu.VMEM((STEPS, block, block), BF16),
            pltpu.VMEM((block, block), F32),
            dma((3,)),
            dma((groups - 1,)),
            dma((groups - 1,)),
            dma((2, cols)),
            dma((2, STEPS)),
            dma((2, groups - 1)),
            dma((2,)),
            dma((STEPS, 3, chunks)),
            dma((STEPS, chunks)),
        ],
        compiler_params=pltpu.CompilerParams(
            collective_id=0, has_side_effects=True, vmem_limit_bytes=52 * 2**20
        ),
    )(front, child_update.reshape(blocks, block, block), send, take)


def solution(mesh):
    in_specs = (P("row", "col"), P("row", "col"), P())
    out_specs = P("row", "col")
    return jax.shard_map(
        on_device, mesh=mesh, in_specs=in_specs, out_specs=out_specs, check_vma=False
    )
```

```python
import functools

import jax
import jax.numpy as jnp
from jax import lax
from jax.experimental import pallas as pl
from jax.experimental.pallas import tpu as pltpu
from jax.sharding import PartitionSpec as P

STEPS = 3
MESH = pl.DeviceIdType.MESH
EXACT = lax.Precision.HIGHEST
F32 = jnp.float32
BF16 = jnp.bfloat16


def dot_t(a, b, precision=None):
    return lax.dot_general(
        a, b, (((1,), (1,)), ((), ())), precision=precision, preferred_element_type=F32
    )


def tables_kernel(groups, blocks, cap, ids_ref, send_ref, take_ref, count_ref):
    me = lax.axis_index("row")
    half = groups // 2
    col_half = lax.axis_index("col") // (lax.axis_size("col") // 2)

    def clear_send(i, _):
        send_ref[i] = 0
        return 0

    def clear_take(i, _):
        take_ref[i] = groups * cap
        return 0

    lax.fori_loop(0, groups * cap, clear_send, 0)
    lax.fori_loop(0, 2 * blocks, clear_take, 0)
    for g in range(groups):
        count_ref[g] = 0
    mine = 2 * (me // half) + col_half
    mine_first = (me % half) * blocks

    def pack(b, _):
        target = lax.div(ids_ref[mine, mine_first + b], jnp.int32(blocks))
        slot = count_ref[target]
        count_ref[target] = slot + 1
        send_ref[target * cap + slot] = b
        return 0

    lax.fori_loop(0, blocks, pack, 0)
    low = me * blocks
    for g in range(groups):
        child = 2 * (g // half) + col_half
        first = (g % half) * blocks

        def take(b, slot):
            local = ids_ref[child, first + b] - low
            here = (local >= 0) & (local < blocks)

            @pl.when(here)
            def _():
                take_ref[(g // half) * blocks + local] = g * cap + slot

            return slot + here.astype(jnp.int32)

        lax.fori_loop(0, blocks, take, jnp.int32(0))


def routes(chips):
    every = (0, 1, 2, 3)
    if chips == 4:
        wide = [(0, 1, every), (0, 2, every), (2, 3, (0, 2)), (1, 3, (1, 3))]
        return [wide, wide, [(1, 3, every), (3, 2, every)]]
    return [
        [(q, q + 1, every) for q in range(p // 2, chips - 1)] for p in range(STEPS)
    ]


def front_kernel(
    groups, cols, blocks, cap, chunk, front_ref, child_ref, send_ref, take_ref, out_ref,
    outgoing, incoming, narrow, top, square, lower, inverse, facing, my_inverse,
    local_sem, ex_send, ex_recv, top_send, top_recv, fac_send, fac_recv, pan_send, pan_recv,
):
    block = 128
    head = STEPS * block
    row = lax.axis_index("row")
    col = lax.axis_index("col")
    chip = col // 2
    core = col % 2
    chunks = blocks * block // chunk
    per_chunk = (blocks + chunks - 1) // chunks

    barrier = pltpu.get_barrier_semaphore()

    def greet_row(o, _):
        pl.semaphore_signal(
            barrier, inc=1, device_id={"row": (row + o) % groups}, device_id_type=MESH
        )
        return 0

    def greet_col(o, _):
        pl.semaphore_signal(
            barrier, inc=1, device_id={"col": (col + o) % cols}, device_id_type=MESH
        )
        return 0

    lax.fori_loop(1, groups, greet_row, 0)
    lax.fori_loop(1, cols, greet_col, 0)
    load = pltpu.make_async_copy(front_ref, out_ref, local_sem.at[0])
    load.start()

    def pack(o, dest):
        base = (row + o) % groups * cap

        def one(s, _):
            dest(s, child_ref[send_ref[base + s]])
            return 0

        lax.fori_loop(0, cap, one, 0)

    def to_self(s, tile):
        incoming[row * cap + s] = tile

    def exchange(o):
        return pltpu.make_async_remote_copy(
            src_ref=outgoing.at[o - 1],
            dst_ref=incoming.at[pl.ds(row * cap, cap)],
            send_sem=ex_send.at[o - 1],
            recv_sem=ex_recv.at[o - 1],
            device_id={"row": (row + o) % groups},
            device_id_type=MESH,
        )

    def top_copies(p, j):
        return [
            pltpu.make_async_remote_copy(
                src_ref=front_ref.at[pl.ds(0, head)],
                dst_ref=top.at[p, pl.ds(0, head)],
                send_sem=top_send.at[0, j],
                recv_sem=top_recv.at[0, p],
                device_id={"col": j},
                device_id_type=MESH,
            ),
            pltpu.make_async_remote_copy(
                src_ref=front_ref.at[pl.ds(pl.multiple_of(j * block, block), block)],
                dst_ref=top.at[p, pl.ds(head, block)],
                send_sem=top_send.at[1, j],
                recv_sem=top_recv.at[1, p],
                device_id={"col": j},
                device_id_type=MESH,
            ),
        ]

    def top_local(p):
        return [
            pltpu.make_async_copy(
                front_ref.at[pl.ds(0, head)], top.at[p, pl.ds(0, head)], local_sem.at[1]
            ),
            pltpu.make_async_copy(
                front_ref.at[pl.ds(pl.multiple_of(col * block, block), block)],
                top.at[p, pl.ds(head, block)],
                local_sem.at[2],
            ),
        ]

    pl.semaphore_wait(barrier, groups - 1 + cols - 1)
    for p in range(STEPS):

        @pl.when((row == 0) & (col == p))
        def _():
            for copy in top_local(p):
                copy.start()

            def send(o, _):
                for copy in top_copies(p, (col + o) % cols):
                    copy.start()
                return 0

            lax.fori_loop(1, cols, send, 0)

    for o in range(1, groups):

        def to_out(s, tile, o=o):
            outgoing[o - 1, s] = tile

        pack(o, to_out)
        exchange(o).start()
    pack(0, to_self)
    incoming[groups * cap] = jnp.zeros((block, block), BF16)

    def give(o, ref, at):
        return pltpu.make_async_remote_copy(
            src_ref=ref,
            dst_ref=ref,
            send_sem=fac_send.at[at, o - 1],
            recv_sem=fac_recv.at[at],
            device_id={"row": o},
            device_id_type=MESH,
        )

    lane = lax.broadcasted_iota(jnp.int32, (block, block), 1)
    sub = lax.broadcasted_iota(jnp.int32, (block, block), 0)

    @pl.when(row == 0)
    def _():
        for p in range(STEPS):

            @pl.when(col == p)
            def _():
                for copy in top_local(p):
                    copy.wait()

            @pl.when(col != p)
            def _():
                for copy in top_copies(p, col):
                    copy.wait_recv()

        my_inverse[...] = jnp.zeros((block, block), F32)
        for k in range(STEPS):
            here = pl.ds(k * block, block)
            corner = top[k, here]
            square[...] = jnp.where(sub >= lane, corner, corner.T)
            inverse[...] = jnp.where(sub == lane, 1.0, 0.0).astype(F32)

            def eliminate(i, _):
                whole = square[...]
                pivot = square[pl.ds(i, 1), :]
                unit = inverse[pl.ds(i, 1), :]
                diag = jnp.sum(jnp.where(lane[:1] == i, pivot, 0.0), axis=1, keepdims=True)
                root = jnp.sqrt(diag)
                pivot = pivot / root
                unit = unit / root
                column = jnp.sum(jnp.where(lane == i, whole, 0.0), axis=1, keepdims=True) / root
                column = jnp.where(sub[:, :1] > i, column, 0.0)
                square[...] = jnp.where(sub == i, pivot, whole - column * pivot)
                inverse[...] = jnp.where(sub == i, unit, inverse[...] - column * unit)
                return 0

            lax.fori_loop(0, block, eliminate, 0)
            inv = inverse[...]

            @pl.when(col == k)
            def _():
                lower[...] = jnp.where(lane >= sub, square[...], 0.0).T
                my_inverse[...] = inv

            rounded = dot_t(top[k], inv, EXACT).astype(BF16)
            facing[k] = rounded[head:]
            for later in range(k + 1, STEPS):
                top[later] = top[later] - dot_t(
                    rounded, rounded[later * block : (later + 1) * block]
                )

        def hand_on(o, _):
            give(o, facing, 0).start()
            give(o, my_inverse, 1).start()
            return 0

        lax.fori_loop(1, groups, hand_on, 0)

    @pl.when(row != 0)
    def _():
        give(1, facing, 0).wait_recv()
        give(1, my_inverse, 1).wait_recv()

    for o in range(1, groups):
        exchange(o).wait_recv()
    load.wait()

    plan = routes(cols // 2)

    def panel_copy(p, c, edge, to):
        part = narrow.at[p, pl.ds(pl.multiple_of(c * chunk, 16), chunk)]
        return pltpu.make_async_remote_copy(
            src_ref=part,
            dst_ref=part,
            send_sem=pan_send.at[p, edge, c],
            recv_sem=pan_recv.at[p, c],
            device_id={"col": to},
            device_id_type=MESH,
        )

    def for_sends(p, c, action):
        @pl.when(core == p % 2)
        def _():
            number = {}
            for source, to, classes in plan[p]:
                edge = number.get(source, 0)
                number[source] = edge + 1
                wanted = chip == source
                if len(classes) < 4:
                    kind = c % 4
                    wanted &= functools.reduce(
                        lambda a, b: a | b, [kind == x for x in classes]
                    )

                @pl.when(wanted)
                def _():
                    action(panel_copy(p, c, edge, to * 2 + core))

            sibling = chip > p // 2 if p % 2 else chip >= p // 2

            @pl.when(sibling)
            def _():
                action(panel_copy(p, c, 2, col + 1 - 2 * core))

    def send(p, c):
        for_sends(p, c, lambda copy: copy.start())

    def arrived(p, c):
        panel_copy(p, c, 0, 0).wait_recv()

    def assemble(c):
        def one(b, _):
            r = c * per_chunk + b

            @pl.when(r < blocks)
            def _():
                at = pl.ds(pl.multiple_of(r * block, block), block)
                out_ref[at] = (
                    out_ref[at]
                    + incoming[take_ref[r]].astype(F32)
                    + incoming[take_ref[blocks + r]].astype(F32)
                )

            return 0

        lax.fori_loop(0, per_chunk, one, 0)

    def update(c, count):
        at = pl.ds(pl.multiple_of(c * chunk, 16), chunk)
        value = out_ref[at]
        for p in range(count):
            value = value - dot_t(narrow[p, at], facing[p])
        return at, value

    def solve(c, p):
        at, value = update(c, p)
        value = dot_t(value, my_inverse[...], EXACT)
        narrow[p, at] = value.astype(BF16)
        out_ref[at] = value
        send(p, c)

    lag = jnp.where(col < 3, 2, jnp.where(col < 4, 4, 5))

    def step(s, _):
        @pl.when(s < chunks)
        def _():
            assemble(s)

            @pl.when(col == 0)
            def _():
                solve(s, 0)

            @pl.when((core == 0) & (col > 0))
            def _():
                arrived(0, s)
                send(0, s)

            @pl.when(col == 1)
            def _():
                arrived(0, s)
                solve(s, 1)

            @pl.when((core == 1) & (col > 1))
            def _():
                arrived(1, s)
                send(1, s)

        c = s - lag

        @pl.when((c >= 0) & (c < chunks))
        def _():
            @pl.when((core == 0) & (col > 1))
            def _():
                arrived(1, c)

            @pl.when((core == 1) & (col > 1))
            def _():
                arrived(0, c)

            @pl.when(col == 2)
            def _():
                solve(c, 2)

            @pl.when(col > 2)
            def _():
                arrived(2, c)

                @pl.when(core == 0)
                def _():
                    send(2, c)

                at, value = update(c, STEPS)
                out_ref[at] = value

        return 0

    lax.fori_loop(0, chunks + 5, step, 0)

    @pl.when(row == 0)
    def _():
        def clear(i, _):
            at = pl.ds(pl.multiple_of(i * block, block), block)

            @pl.when(i < col)
            def _():
                out_ref[at] = jnp.zeros((block, block), F32)

            @pl.when((i == col) & (col < STEPS))
            def _():
                out_ref[at] = lower[...]

            @pl.when((i == col) & (col >= STEPS))
            def _():
                out_ref[at] = jnp.where(sub >= lane, out_ref[at], 0.0)

            return 0

        lax.fori_loop(0, cols, clear, 0)

    for o in range(1, groups):
        exchange(o).wait_send()

    @pl.when(row == 0)
    def _():
        def gone(o, _):
            give(o, facing, 0).wait_send()
            give(o, my_inverse, 1).wait_send()
            return 0

        lax.fori_loop(1, groups, gone, 0)
        for p in range(STEPS):

            @pl.when(col == p)
            def _():
                def left(o, _):
                    for copy in top_copies(p, (col + o) % cols):
                        copy.wait_send()
                    return 0

                lax.fori_loop(1, cols, left, 0)

    def drain(c, _):
        for p in range(STEPS):

            @pl.when(col >= p)
            def _():
                for_sends(p, c, lambda copy: copy.wait_send())

        return 0

    lax.fori_loop(0, chunks, drain, 0)


def on_device(front, child_update, child_rows):
    rows, block = front.shape
    groups = lax.axis_size("row")
    cols = lax.axis_size("col")
    blocks = rows // block
    cap = (blocks + groups - 1) // groups
    chunk = max(c for c in range(16, 2049, 16) if rows % c == 0)
    chunks = rows // chunk
    send, take = pl.pallas_call(
        functools.partial(tables_kernel, groups, blocks, cap),
        out_shape=(
            jax.ShapeDtypeStruct((groups * cap,), jnp.int32),
            jax.ShapeDtypeStruct((2 * blocks,), jnp.int32),
        ),
        in_specs=[pl.BlockSpec(memory_space=pltpu.SMEM)],
        out_specs=(
            pl.BlockSpec(memory_space=pltpu.SMEM),
            pl.BlockSpec(memory_space=pltpu.SMEM),
        ),
        scratch_shapes=[pltpu.SMEM((groups,), jnp.int32)],
    )(child_rows)
    dma = pltpu.SemaphoreType.DMA
    return pl.pallas_call(
        functools.partial(front_kernel, groups, cols, blocks, cap, chunk),
        out_shape=jax.ShapeDtypeStruct((rows, block), F32),
        in_specs=[
            pl.BlockSpec(memory_space=pl.ANY),
            pl.BlockSpec(memory_space=pltpu.VMEM),
            pl.BlockSpec(memory_space=pltpu.SMEM),
            pl.BlockSpec(memory_space=pltpu.SMEM),
        ],
        out_specs=pl.BlockSpec(memory_space=pltpu.VMEM),
        scratch_shapes=[
            pltpu.VMEM((groups - 1, cap, block, block), BF16),
            pltpu.VMEM((groups * cap + 1, block, block), BF16),
            pltpu.VMEM((STEPS, rows, block), BF16),
            pltpu.VMEM((STEPS, (STEPS + 1) * block, block), F32),
            pltpu.VMEM((block, block), F32),
            pltpu.VMEM((block, block), F32),
            pltpu.VMEM((block, block), F32),
            pltpu.VMEM((STEPS, block, block), BF16),
            pltpu.VMEM((block, block), F32),
            dma((3,)),
            dma((groups - 1,)),
            dma((groups - 1,)),
            dma((2, cols)),
            dma((2, STEPS)),
            dma((2, groups - 1)),
            dma((2,)),
            dma((STEPS, 3, chunks)),
            dma((STEPS, chunks)),
        ],
        compiler_params=pltpu.CompilerParams(
            collective_id=0, has_side_effects=True, vmem_limit_bytes=52 * 2**20
        ),
    )(front, child_update.reshape(blocks, block, block), send, take)


def solution(mesh):
    in_specs = (P("row", "col"), P("row", "col"), P())
    out_specs = P("row", "col")
    return jax.shard_map(
        on_device, mesh=mesh, in_specs=in_specs, out_specs=out_specs, check_vma=False
    )
```
